32 devices in a mesh: snp: 4 (over z), tile: 8 (over y, x, core).
Axes of the slice: x: 2, y: 2, z: 4, core: 2. Of those that a mesh axis runs over, the one named last changes fastest.
Arguments:
- dosages: float32 [16384, 8192], P('tile', 'snp'), may hold values from 0 to 2
- phenotypes: float32 [16384, 512], P('tile', 'snp'), may hold values from -6 to 6
Outputs:
- factor: float32 [16384, 512], P('tile')
- whitened: float32 [16384, 512], P('tile', 'snp')
The draws below stay inside these ranges and needn't reach their ends.
All inputs are finite; a program needn't handle non-finite values.
Results may differ from the reference program's by a relative error of at most 0.00011.
Values sent between devices are 32-bit elements; how exact they have to be, the bound alone decides.
A program may use at most 128 MiB of HBM per device.

```python
import jax
import jax.numpy as jnp
from jax import lax

ROWS_DEV = 2048
BLK = 256
PHENO = 512
NSAMP = 16384
NSNP = 8192


def draw_dosages(key, part):
    base = jax.random.randint(jax.random.fold_in(key, 1), (1, NSNP), 5, 331)
    sample_ids = jnp.arange(NSAMP, dtype=jnp.int32)[:, None]
    threshold = base * (NSAMP + 2 * sample_ids) // NSAMP
    first_allele = jax.random.randint(jax.random.fold_in(key, 2), (NSAMP, NSNP), 0, 1000) < threshold
    second_allele = jax.random.randint(jax.random.fold_in(key, 3), (NSAMP, NSNP), 0, 1000) < threshold
    top = 0.3
    ramp = (NSAMP + 2 * sample_ids).astype(jnp.float32) / (3.0 * NSAMP)
    first_error = jax.random.uniform(jax.random.fold_in(key, 4), (NSAMP, NSNP), jnp.float32, 0.0, top) * ramp
    second_error = jax.random.uniform(jax.random.fold_in(key, 5), (NSAMP, NSNP), jnp.float32, 0.0, top) * ramp
    first_value = jnp.where(first_allele, 1.0 - first_error, first_error)
    second_value = jnp.where(second_allele, 1.0 - second_error, second_error)
    return (first_value + second_value).astype(jnp.float32)


def levels(stream_key, dims, split, least, largest):
    level, own = 1.0, jax.random.fold_in(stream_key, 6)
    for dim, blocks in split:
        steps = jnp.exp(jax.random.uniform(jax.random.fold_in(own, dim), (blocks,), jnp.float32, least / len(split), largest / len(split)))
        level = level * jnp.repeat(steps, dims[dim] // blocks).reshape([-1 if axis == dim else 1 for axis in range(len(dims))])
    return level


def scatter_about(rng, dims, deviation, most, pieces=(), kind=jnp.bfloat16):
    array = deviation * jax.random.normal(rng, dims, jnp.float32)
    if pieces:
        array = array * levels(rng, dims, pieces, -0.22, 0.18)
    return jnp.clip(array, -most, most).astype(kind)


def setup_inputs(seed: int = 0) -> dict:
    splits = jax.random.split(jax.random.key(seed), 3)
    return {
        "dosages": draw_dosages(jax.random.fold_in(splits[2], 71), 0),
        "phenotypes": scatter_about(splits[1], (NSAMP, PHENO), 1.0, 6.0, ((0, 8), (1, 4)), jnp.float32),
    }


def right_solve(lower, values):
    return lax.linalg.triangular_solve(lower, values, left_side=False, lower=True, transpose_a=True)

def left_solve(lower, values):
    return lax.linalg.triangular_solve(lower, values, left_side=True, lower=True)

def reference(dosages, phenotypes):
    n_rows = dosages.shape[0]
    n_snps = dosages.shape[1]
    counts = lax.optimization_barrier(jnp.sum(dosages, axis=0))
    allele_freq = counts / (2.0 * n_rows)
    spread = jnp.maximum(2.0 * allele_freq * (1.0 - allele_freq), 0.05)
    standard = (dosages - 2.0 * allele_freq) * lax.rsqrt(spread)
    stacked = jnp.concatenate([standard[:BLK], standard[ROWS_DEV:ROWS_DEV + BLK]], 0)
    cross = lax.dot_general(standard.astype(jnp.float32), stacked.astype(jnp.float32), (((1,), (1,)), ((), ())), precision=lax.Precision.HIGHEST, preferred_element_type=jnp.float32) * (1.0 / n_snps)
    diag = jnp.concatenate([cross[:BLK], cross[ROWS_DEV:ROWS_DEV + BLK]], 0) + jnp.eye(2 * BLK, dtype=jnp.float32)
    first_diag = jnp.linalg.cholesky(diag[:BLK, :BLK])
    lower_left = right_solve(first_diag, diag[BLK:, :BLK])
    schur = diag[BLK:, BLK:] - jnp.dot(lower_left, lower_left.T, precision=lax.Precision.HIGHEST)
    second_diag = jnp.linalg.cholesky(schur)
    left = right_solve(first_diag, cross[:, :BLK])
    rest = cross[:, BLK:] - jnp.dot(left, lower_left.T, precision=lax.Precision.HIGHEST)
    right = right_solve(second_diag, rest)
    left = left.at[:BLK].set(first_diag).at[ROWS_DEV:ROWS_DEV + BLK].set(lower_left)
    right = right.at[:BLK].set(jnp.zeros((BLK, BLK), jnp.float32)).at[ROWS_DEV:ROWS_DEV + BLK].set(second_diag)
    first_solved = left_solve(first_diag, phenotypes[:BLK])
    updated = phenotypes - jnp.dot(left, first_solved, precision=lax.Precision.HIGHEST)
    updated = updated.at[:BLK].set(first_solved)
    second_solved = left_solve(second_diag, updated[ROWS_DEV:ROWS_DEV + BLK])
    whitened = updated - jnp.dot(right, second_solved, precision=lax.Precision.HIGHEST)
    whitened = whitened.at[ROWS_DEV:ROWS_DEV + BLK].set(second_solved)
    return (jnp.concatenate([left, right], 1), whitened)
```

```python
import functools

import jax
import jax.numpy as jnp
from jax import lax
from jax.experimental import pallas as pl
from jax.experimental.pallas import tpu as pltpu
from jax.sharding import PartitionSpec as P

BLK = 256
HALF = BLK // 2
PIECES = 16
CHUNK = 64
MROWS = 256
MESH = pl.DeviceIdType.MESH
NT = (((1,), (1,)), ((), ()))


def split(value):
    high = value.astype(jnp.bfloat16)
    return high, (value - high.astype(jnp.float32)).astype(jnp.bfloat16)


def kernel(n_tile, n_snp, dos_hbm, phe_hbm, cross_hbm, diag_hbm, heads_hbm,
           dos, panels, heads, diag, high, low, counts, mean, scale, x, oin, iin,
           load_sem, head_sem, out_sem, cnt_send, cnt_recv,
           a_send, a_recv, b_send, b_recv, sa_send, sa_recv, sb_send, sb_recv,
           da_send, da_recv, db_send, db_recv, ea_send, ea_recv, eb_send, eb_recv,
           i_send, o_recv, o_send, i_recv):
    rows, snps = dos.shape
    wide = 2 * BLK
    tile = lax.axis_index("tile")
    snp = lax.axis_index("snp")
    chips = n_tile // 2
    across = chips // 2
    core = lax.rem(tile, 2)
    chip = lax.div(tile, 2)
    pos = jnp.where(chip < across, chip, chips + across - 1 - chip)
    sib = chip * 2 + 1 - core

    def at_pos(q):
        q = lax.rem(q + chips, chips)
        return 2 * jnp.where(q < across, q, chips + across - 1 - q) + core

    right, left = at_pos(pos + 1), at_pos(pos - 1)
    half = n_snp // 2
    lower = snp < half
    depth = jnp.where(lower, snp, n_snp - 1 - snp)
    inner = jnp.where(lower, snp + 1, snp - 1)
    outer = jnp.where(lower, snp - 1, snp + 1)
    middle = depth == half - 1
    has_outer = depth > 0

    barrier = pltpu.get_barrier_semaphore()
    for d in range(1, n_tile):
        pl.semaphore_signal(barrier, inc=1, device_id={"tile": lax.rem(tile + d, n_tile)}, device_id_type=MESH)
    pl.semaphore_signal(barrier, inc=1, device_id={"snp": inner}, device_id_type=MESH)

    @pl.when(has_outer)
    def _():
        pl.semaphore_signal(barrier, inc=1, device_id={"snp": outer}, device_id_type=MESH)

    def load(k):
        r = pl.ds(pl.multiple_of(k * MROWS, MROWS), MROWS)
        return pltpu.make_async_copy(dos_hbm.at[r], dos.at[r], load_sem.at[k])

    n_load = rows // MROWS
    own = pl.ds(pl.multiple_of(core * BLK, BLK), BLK)
    own_panel = pltpu.make_async_copy(dos_hbm.at[pl.ds(0, BLK)], panels.at[own], head_sem.at[0])
    own_heads = pltpu.make_async_copy(phe_hbm.at[pl.ds(0, BLK)], heads.at[own], head_sem.at[1])

    @pl.when(pos == 0)
    def _():
        own_panel.start()
        own_heads.start()

    for k in range(n_load):
        load(k).start()
    pl.semaphore_wait(barrier, n_tile + jnp.where(has_outer, 1, 0))

    @pl.when(pos == 0)
    def _():
        own_panel.wait()
        own_heads.wait()

    def remote(ref, send, recv, **where):
        return pltpu.make_async_remote_copy(src_ref=ref, dst_ref=ref, send_sem=send, recv_sem=recv,
                                            device_id=where, device_id_type=MESH)

    def piece(buf, which, side, k, size):
        return buf.at[pl.ds(pl.multiple_of(which * BLK + side * HALF + k * size, size), size)]

    def ring_step(buf, size, sems, k_a, k_b, last, index_a, index_b):
        (asn, arc, bsn, brc, sas, sar, sbs, sbr) = sems

        @pl.when((k_a >= 0) & (k_a < last))
        def _():
            ref = piece(buf, core, 0, k_a, size)
            i = index_a
            d = remote(ref, asn.at[i], arc.at[i], tile=right)

            @pl.when(pos > 0)
            def _():
                d.wait_recv()

            @pl.when(pos < chips - 1)
            def _():
                d.start()

            remote(ref, sas.at[i], sar.at[i], tile=sib).start()

        @pl.when((k_b >= 0) & (k_b < last))
        def _():
            ref = piece(buf, core, 1, k_b, size)
            i = index_b
            d = remote(ref, bsn.at[i], brc.at[i], tile=left)

            @pl.when(pos > 0)
            def _():
                d.wait_recv()

            @pl.when(pos != 1)
            def _():
                d.start()

            remote(ref, sbs.at[i], sbr.at[i], tile=sib).start()

    def sibling_wait(buf, size, sems, k, i):
        (asn, arc, bsn, brc, sas, sar, sbs, sbr) = sems
        remote(piece(buf, 1 - core, 0, k, size), sas.at[i], sar.at[i], tile=sib).wait_recv()
        remote(piece(buf, 1 - core, 1, k, size), sbs.at[i], sbr.at[i], tile=sib).wait_recv()

    def drain(buf, size, sems, k, i):
        (asn, arc, bsn, brc, sas, sar, sbs, sbr) = sems
        ref_a, ref_b = piece(buf, core, 0, k, size), piece(buf, core, 1, k, size)

        @pl.when(pos < chips - 1)
        def _():
            remote(ref_a, asn.at[i], arc.at[i], tile=right).wait_send()

        @pl.when(pos != 1)
        def _():
            remote(ref_b, bsn.at[i], brc.at[i], tile=left).wait_send()

        remote(ref_a, sas.at[i], sar.at[i], tile=sib).wait_send()
        remote(ref_b, sbs.at[i], sbr.at[i], tile=sib).wait_send()

    ring = (a_send, a_recv, b_send, b_recv, sa_send, sa_recv, sb_send, sb_recv)
    dring = (da_send, da_recv, db_send, db_recv, ea_send, ea_recv, eb_send, eb_recv)
    psize = HALF // PIECES
    start_b = lax.rem(chips - pos, chips)

    def count_copy(d):
        ref = counts.at[tile]
        return remote(ref, cnt_send.at[d], cnt_recv.at[tile], tile=lax.rem(tile + d, n_tile))

    def ring_slot(s, total):
        @pl.when(s < n_load)
        def _():
            load(s).wait()
        r = jnp.minimum(s, n_load - 1)
        part = jnp.sum(dos[pl.ds(pl.multiple_of(r * MROWS, MROWS), MROWS)].reshape(MROWS // 8, 8, snps), axis=0)
        total = total + jnp.where(s < n_load, part, 0.0)
        ring_step(panels, psize, ring, s - pos, s - start_b, PIECES, s - pos, s - start_b)
        return total

    total = lax.fori_loop(0, n_load, ring_slot, jnp.zeros((8, snps), jnp.float32))
    counts[tile] = jnp.sum(total, axis=0, keepdims=True)
    for d in range(1, n_tile):
        count_copy(d).start()

    def ring_rest(s, carry):
        ring_step(panels, psize, ring, s - pos, s - start_b, PIECES, s - pos, s - start_b)
        return carry

    lax.fori_loop(n_load, PIECES + chips, ring_rest, 0)
    for d in range(1, n_tile):
        source = lax.rem(tile + d, n_tile)
        remote(counts.at[source], cnt_send.at[d], cnt_recv.at[source], tile=source).wait_recv()
    freq = counts[0]
    for t in range(1, n_tile):
        freq = freq + counts[t]
    freq = freq / (2.0 * rows * n_tile)
    mean[...] = 2.0 * freq
    scale[...] = lax.rsqrt(jnp.maximum(2.0 * freq * (1.0 - freq), 0.05))
    ring_step(heads, HALF, ring, 0, jnp.where(pos == 0, 0, -1), 1, PIECES, PIECES)

    @pl.when(pos > 0)
    def _():
        ring_step(heads, HALF, ring, -1, 0, 1, PIECES, PIECES)

    def wait_sib(k, carry):
        sibling_wait(panels, psize, ring, k, k)
        return carry

    lax.fori_loop(0, PIECES, wait_sib, 0)

    def standardize(k, carry):
        r = pl.ds(pl.multiple_of(k * 64, 64), 64)
        h, l = split((panels[r] - mean[...]) * scale[...])
        high[r] = h
        low[r] = l
        return carry

    lax.fori_loop(0, wide // 64, standardize, 0)

    n_chunk = rows // CHUNK
    per = MROWS // CHUNK
    inverse_count = 1.0 / (snps * n_snp)

    def rows_of(buf, k):
        return buf.at[pl.ds(pl.multiple_of(k * CHUNK, CHUNK), CHUNK)]

    def to_inner(k):
        return [
            pltpu.make_async_remote_copy(src_ref=rows_of(x, k), dst_ref=rows_of(dst, k), send_sem=i_send.at[k],
                                         recv_sem=recv.at[k], device_id={"snp": inner}, device_id_type=MESH)
            for dst, recv in ((oin, o_recv), (iin, i_recv))
        ]

    def to_outer(k):
        return remote(rows_of(iin, k), o_send.at[k], i_recv.at[k], snp=outer)

    def to_hbm(k):
        return pltpu.make_async_copy(rows_of(iin, k), rows_of(cross_hbm, k), out_sem.at[k])

    b_shift = half + (half - 1 - depth)
    heads_d = BLK // CHUNK
    dsize = HALF // heads_d

    def slot(s, carry):
        @pl.when((lax.rem(s, per) == 0) & (s < n_chunk))
        def _():
            r = pl.ds(pl.multiple_of(lax.div(s, per) * MROWS, MROWS), MROWS)
            h, l = split((dos[r] - mean[...]) * scale[...])
            dot = functools.partial(lax.dot_general, dimension_numbers=NT, preferred_element_type=jnp.float32)
            x[r] = (dot(h, high[...]) + (dot(h, low[...]) + dot(l, high[...]))) * inverse_count

        k_a = s - depth

        @pl.when((k_a >= 0) & (k_a < n_chunk))
        def _():
            plain, across_copy = to_inner(k_a)

            @pl.when(has_outer)
            def _():
                plain.wait_recv()
                r = pl.ds(pl.multiple_of(k_a * CHUNK, CHUNK), CHUNK)
                x[r] = x[r] + oin[r]

            @pl.when(middle)
            def _():
                across_copy.start()

            @pl.when(jnp.logical_not(middle))
            def _():
                plain.start()

        k_b = s - b_shift

        @pl.when((k_b >= 0) & (k_b < n_chunk))
        def _():
            to_outer(k_b).wait_recv()

            @pl.when(middle)
            def _():
                r = pl.ds(pl.multiple_of(k_b * CHUNK, CHUNK), CHUNK)
                iin[r] = x[r] + iin[r]

            @pl.when(has_outer)
            def _():
                to_outer(k_b).start()

            to_hbm(k_b).start()

            @pl.when((k_b < heads_d) & (pos == 0))
            def _():
                r = pl.ds(pl.multiple_of(k_b * CHUNK, CHUNK), CHUNK)
                diag[pl.ds(pl.multiple_of(core * BLK + k_b * CHUNK, CHUNK), CHUNK)] = iin[r]

        k_d = s - b_shift - heads_d
        ring_step(diag, dsize, dring, k_d - pos, k_d - start_b, heads_d, k_d - pos, k_d - start_b)
        return carry

    lax.fori_loop(0, n_chunk + 2 * half, slot, 0)
    for k in range(heads_d):
        sibling_wait(diag, dsize, dring, k, k)
    sibling_wait(heads, HALF, ring, 0, PIECES)
    out_d = pltpu.make_async_copy(diag, diag_hbm, head_sem.at[0])
    out_h = pltpu.make_async_copy(heads, heads_hbm, head_sem.at[1])
    out_d.start()
    out_h.start()

    def finish(k, carry):
        to_inner(k)[0].wait_send()

        @pl.when(has_outer)
        def _():
            to_outer(k).wait_send()

        to_hbm(k).wait()
        return carry

    lax.fori_loop(0, n_chunk, finish, 0)

    def drain_ring(k, carry):
        drain(panels, psize, ring, k, k)
        return carry

    lax.fori_loop(0, PIECES, drain_ring, 0)
    drain(heads, HALF, ring, 0, PIECES)
    for k in range(heads_d):
        drain(diag, dsize, dring, k, k)
    for d in range(1, n_tile):
        count_copy(d).wait_send()
    out_d.wait()
    out_h.wait()


def right_solve(lower, values):
    return lax.linalg.triangular_solve(lower, values, left_side=False, lower=True, transpose_a=True)


def left_solve(lower, values):
    return lax.linalg.triangular_solve(lower, values, left_side=True, lower=True)


def gather_cross(dosages, phenotypes, n_tile, n_snp):
    rows, snps = dosages.shape
    wide = 2 * BLK
    f32 = jnp.float32
    n_chunk = rows // CHUNK
    dma = pltpu.SemaphoreType.DMA
    return pl.pallas_call(
        functools.partial(kernel, n_tile, n_snp),
        out_shape=(
            jax.ShapeDtypeStruct((rows, wide), f32),
            jax.ShapeDtypeStruct((wide, wide), f32),
            jax.ShapeDtypeStruct((wide, phenotypes.shape[1]), f32),
        ),
        in_specs=[pl.BlockSpec(memory_space=pl.ANY)] * 2,
        out_specs=[pl.BlockSpec(memory_space=pl.ANY)] * 3,
        scratch_shapes=[
            pltpu.VMEM((rows, snps), f32),
            pltpu.VMEM((wide, snps), f32),
            pltpu.VMEM((wide, phenotypes.shape[1]), f32),
            pltpu.VMEM((wide, wide), f32),
            pltpu.VMEM((wide, snps), jnp.bfloat16),
            pltpu.VMEM((wide, snps), jnp.bfloat16),
            pltpu.VMEM((n_tile, 1, snps), f32),
            pltpu.VMEM((1, snps), f32),
            pltpu.VMEM((1, snps), f32),
            pltpu.VMEM((rows, wide), f32),
            pltpu.VMEM((rows, wide), f32),
            pltpu.VMEM((rows, wide), f32),
            dma((rows // MROWS,)),
            dma((2,)),
            dma((n_chunk,)),
            dma((n_tile,)),
            dma((n_tile,)),
        ]
        + [dma((PIECES + 1,))] * 8
        + [dma((BLK // CHUNK,))] * 8
        + [dma((n_chunk,))] * 4,
        compiler_params=pltpu.CompilerParams(
            collective_id=0, has_side_effects=True, vmem_limit_bytes=58 * 1024 * 1024
        ),
    )(dosages, phenotypes)


def body(dosages, phenotypes):
    width = BLK
    n_tile = lax.axis_size("tile")
    n_snp = lax.axis_size("snp")
    tile_index = lax.axis_index("tile")
    cross, diag, heads = gather_cross(dosages, phenotypes, n_tile, n_snp)
    diag = diag + jnp.eye(2 * width, dtype=jnp.float32)
    first_diag = jnp.linalg.cholesky(diag[:width, :width])
    lower_left = right_solve(first_diag, diag[width:, :width])
    schur = diag[width:, width:] - jnp.dot(
        lower_left, lower_left.T, precision=lax.Precision.HIGHEST
    )
    second_diag = jnp.linalg.cholesky(schur)
    left_part = right_solve(first_diag, cross[:, :width])
    rest = cross[:, width:] - jnp.dot(left_part, lower_left.T, precision=lax.Precision.HIGHEST)
    factor = jnp.concatenate([left_part, right_solve(second_diag, rest)], 1)
    first_rows = jnp.concatenate([first_diag, jnp.zeros((width, width), jnp.float32)], 1)
    second_rows = jnp.concatenate([lower_left, second_diag], 1)
    head_rows = jnp.where(
        tile_index == 0, first_rows, jnp.where(tile_index == 1, second_rows, factor[:width])
    )
    factor = factor.at[:width].set(head_rows)
    first_solved = left_solve(first_diag, heads[:width])
    second_head = heads[width:] - jnp.dot(lower_left, first_solved, precision=lax.Precision.HIGHEST)
    second_solved = left_solve(second_diag, second_head)
    solved = jnp.concatenate([first_solved, second_solved], 0)
    current = phenotypes - jnp.dot(factor, solved, precision=lax.Precision.HIGHEST)
    current = current.at[:width].set(
        jnp.where(tile_index == 0, first_solved, jnp.where(tile_index == 1, second_solved, current[:width]))
    )
    return (factor, current)


def solution(mesh):
    placed = (P("tile", "snp"), P("tile", "snp"))
    return jax.shard_map(
        body,
        mesh=mesh,
        in_specs=placed,
        out_specs=(P("tile", None), P("tile", "snp")),
        check_vma=False,
    )
```

```python
import functools

import jax
import jax.numpy as jnp
from jax import lax
from jax.experimental import pallas as pl
from jax.experimental.pallas import tpu as pltpu
from jax.sharding import PartitionSpec as P

BLK = 256
HALF = BLK // 2
PIECES = 16
CHUNK = 64
MROWS = 256
SLAB = 64
MESH = pl.DeviceIdType.MESH
NT = (((1,), (1,)), ((), ()))


def split(value):
    high = value.astype(jnp.bfloat16)
    return high, (value - high.astype(jnp.float32)).astype(jnp.bfloat16)


def eliminate(work, first, last):
    below = lax.broadcasted_iota(jnp.int32, (SLAB, 1), 0)
    for j in range(first, last):
        column = jnp.where(below > j, work[:, j:j + 1], 0.0)
        work = work - column * (work[j:j + 1] * (1.0 / work[j:j + 1, j:j + 1]))
    return work


def slab_update(b, work, inverse, upper):
    wide = inverse.shape[0]
    exact = functools.partial(jnp.dot, precision=lax.Precision.HIGHEST, preferred_element_type=jnp.float32)
    r = lax.broadcasted_iota(jnp.int32, work.shape, 0)
    c = lax.broadcasted_iota(jnp.int32, work.shape, 1)
    pivots = jnp.sum(jnp.where(r == c, work, 0.0), axis=1, keepdims=True)
    work = work * lax.rsqrt(pivots)
    own = pl.ds(pl.multiple_of(b * SLAB, SLAB), SLAB)
    lane = lax.broadcasted_iota(jnp.int32, (SLAB, wide), 1)
    mine = (lane >= b * SLAB) & (lane < (b + 1) * SLAB)
    after = lane >= (b + 1) * SLAB
    upper_block = jnp.where(c < SLAB, jnp.where(c >= r, work, 0.0), 0.0)[:, :SLAB]
    inverse_block = work[:, SLAB:]
    repeat = wide // SLAB
    solved = exact(inverse_block, inverse[own])
    solved = jnp.where(mine, jnp.concatenate([inverse_block] * repeat, 1), solved)
    later = jnp.where(after, solved, 0.0)
    upper[own] = jnp.where(mine, jnp.concatenate([upper_block] * repeat, 1), later)
    inverse[own] = solved
    row_all = lax.broadcasted_iota(jnp.int32, (wide, wide), 0)
    lane_all = lax.broadcasted_iota(jnp.int32, (wide, wide), 1)
    cleared = (row_all >= (b + 1) * SLAB) & (lane_all >= b * SLAB) & (lane_all < (b + 1) * SLAB)
    inverse[...] = jnp.where(cleared, 0.0, inverse[...]) - exact(later.T, solved)


def kernel(n_tile, n_snp, dos_hbm, phe_hbm, cross_hbm, inverse_hbm, upper_hbm, heads_hbm,
           dos, panels, heads, diag, inverse, upper, work, high, low, counts, mean, scale, x, oin, iin,
           load_sem, head_sem, out_sem, cnt_send, cnt_recv,
           a_send, a_recv, b_send, b_recv, sa_send, sa_recv, sb_send, sb_recv,
           da_send, da_recv, db_send, db_recv, ea_send, ea_recv, eb_send, eb_recv,
           i_send, o_recv, o_send, i_recv):
    rows, snps = dos.shape
    wide = 2 * BLK
    tile = lax.axis_index("tile")
    snp = lax.axis_index("snp")
    chips = n_tile // 2
    across = chips // 2
    core = lax.rem(tile, 2)
    chip = lax.div(tile, 2)
    pos = jnp.where(chip < across, chip, chips + across - 1 - chip)
    sib = chip * 2 + 1 - core

    def at_pos(q):
        q = lax.rem(q + chips, chips)
        return 2 * jnp.where(q < across, q, chips + across - 1 - q) + core

    right, left = at_pos(pos + 1), at_pos(pos - 1)
    half = n_snp // 2
    lower = snp < half
    depth = jnp.where(lower, snp, n_snp - 1 - snp)
    inner = jnp.where(lower, snp + 1, snp - 1)
    outer = jnp.where(lower, snp - 1, snp + 1)
    middle = depth == half - 1
    has_outer = depth > 0

    barrier = pltpu.get_barrier_semaphore()
    for d in range(1, n_tile):
        pl.semaphore_signal(barrier, inc=1, device_id={"tile": lax.rem(tile + d, n_tile)}, device_id_type=MESH)
    pl.semaphore_signal(barrier, inc=1, device_id={"snp": inner}, device_id_type=MESH)

    @pl.when(has_outer)
    def _():
        pl.semaphore_signal(barrier, inc=1, device_id={"snp": outer}, device_id_type=MESH)

    def load(k):
        r = pl.ds(pl.multiple_of(k * MROWS, MROWS), MROWS)
        return pltpu.make_async_copy(dos_hbm.at[r], dos.at[r], load_sem.at[k])

    n_load = rows // MROWS
    own = pl.ds(pl.multiple_of(core * BLK, BLK), BLK)
    own_panel = pltpu.make_async_copy(dos_hbm.at[pl.ds(0, BLK)], panels.at[own], head_sem.at[0])
    own_heads = pltpu.make_async_copy(phe_hbm.at[pl.ds(0, BLK)], heads.at[own], head_sem.at[1])

    @pl.when(pos == 0)
    def _():
        own_panel.start()
        own_heads.start()

    for k in range(n_load):
        load(k).start()
    pl.semaphore_wait(barrier, n_tile + jnp.where(has_outer, 1, 0))

    @pl.when(pos == 0)
    def _():
        own_panel.wait()
        own_heads.wait()

    def remote(ref, send, recv, **where):
        return pltpu.make_async_remote_copy(src_ref=ref, dst_ref=ref, send_sem=send, recv_sem=recv,
                                            device_id=where, device_id_type=MESH)

    def piece(buf, which, side, k, size):
        return buf.at[pl.ds(pl.multiple_of(which * BLK + side * HALF + k * size, size), size)]

    def ring_step(buf, size, sems, k_a, k_b, last, index_a, index_b):
        (asn, arc, bsn, brc, sas, sar, sbs, sbr) = sems

        @pl.when((k_a >= 0) & (k_a < last))
        def _():
            ref = piece(buf, core, 0, k_a, size)
            i = index_a
            d = remote(ref, asn.at[i], arc.at[i], tile=right)

            @pl.when(pos > 0)
            def _():
                d.wait_recv()

            @pl.when(pos < chips - 1)
            def _():
                d.start()

            remote(ref, sas.at[i], sar.at[i], tile=sib).start()

        @pl.when((k_b >= 0) & (k_b < last))
        def _():
            ref = piece(buf, core, 1, k_b, size)
            i = index_b
            d = remote(ref, bsn.at[i], brc.at[i], tile=left)

            @pl.when(pos > 0)
            def _():
                d.wait_recv()

            @pl.when(pos != 1)
            def _():
                d.start()

            remote(ref, sbs.at[i], sbr.at[i], tile=sib).start()

    def sibling_wait(buf, size, sems, k, i):
        (asn, arc, bsn, brc, sas, sar, sbs, sbr) = sems
        remote(piece(buf, 1 - core, 0, k, size), sas.at[i], sar.at[i], tile=sib).wait_recv()
        remote(piece(buf, 1 - core, 1, k, size), sbs.at[i], sbr.at[i], tile=sib).wait_recv()

    def drain(buf, size, sems, k, i):
        (asn, arc, bsn, brc, sas, sar, sbs, sbr) = sems
        ref_a, ref_b = piece(buf, core, 0, k, size), piece(buf, core, 1, k, size)

        @pl.when(pos < chips - 1)
        def _():
            remote(ref_a, asn.at[i], arc.at[i], tile=right).wait_send()

        @pl.when(pos != 1)
        def _():
            remote(ref_b, bsn.at[i], brc.at[i], tile=left).wait_send()

        remote(ref_a, sas.at[i], sar.at[i], tile=sib).wait_send()
        remote(ref_b, sbs.at[i], sbr.at[i], tile=sib).wait_send()

    ring = (a_send, a_recv, b_send, b_recv, sa_send, sa_recv, sb_send, sb_recv)
    dring = (da_send, da_recv, db_send, db_recv, ea_send, ea_recv, eb_send, eb_recv)
    psize = HALF // PIECES
    start_b = lax.rem(chips - pos, chips)

    def count_copy(d):
        ref = counts.at[tile]
        return remote(ref, cnt_send.at[d], cnt_recv.at[tile], tile=lax.rem(tile + d, n_tile))

    def ring_slot(s, total):
        @pl.when(s < n_load)
        def _():
            load(s).wait()
        r = jnp.minimum(s, n_load - 1)
        part = jnp.sum(dos[pl.ds(pl.multiple_of(r * MROWS, MROWS), MROWS)].reshape(MROWS // 8, 8, snps), axis=0)
        total = total + jnp.where(s < n_load, part, 0.0)
        ring_step(panels, psize, ring, s - pos, s - start_b, PIECES, s - pos, s - start_b)
        return total

    total = lax.fori_loop(0, n_load, ring_slot, jnp.zeros((8, snps), jnp.float32))
    counts[tile] = jnp.sum(total, axis=0, keepdims=True)
    for d in range(1, n_tile):
        count_copy(d).start()

    def ring_rest(s, carry):
        ring_step(panels, psize, ring, s - pos, s - start_b, PIECES, s - pos, s - start_b)
        return carry

    lax.fori_loop(n_load, PIECES + chips, ring_rest, 0)
    for d in range(1, n_tile):
        source = lax.rem(tile + d, n_tile)
        remote(counts.at[source], cnt_send.at[d], cnt_recv.at[source], tile=source).wait_recv()
    freq = counts[0]
    for t in range(1, n_tile):
        freq = freq + counts[t]
    freq = freq / (2.0 * rows * n_tile)
    mean[...] = 2.0 * freq
    scale[...] = lax.rsqrt(jnp.maximum(2.0 * freq * (1.0 - freq), 0.05))
    ring_step(heads, HALF, ring, 0, jnp.where(pos == 0, 0, -1), 1, PIECES, PIECES)

    @pl.when(pos > 0)
    def _():
        ring_step(heads, HALF, ring, -1, 0, 1, PIECES, PIECES)

    def wait_sib(k, carry):
        sibling_wait(panels, psize, ring, k, k)
        return carry

    lax.fori_loop(0, PIECES, wait_sib, 0)

    def standardize(k, carry):
        r = pl.ds(pl.multiple_of(k * 64, 64), 64)
        h, l = split((panels[r] - mean[...]) * scale[...])
        high[r] = h
        low[r] = l
        return carry

    lax.fori_loop(0, wide // 64, standardize, 0)

    n_chunk = rows // CHUNK
    per = MROWS // CHUNK
    inverse_count = 1.0 / (snps * n_snp)

    def rows_of(buf, k):
        return buf.at[pl.ds(pl.multiple_of(k * CHUNK, CHUNK), CHUNK)]

    def to_inner(k):
        return [
            pltpu.make_async_remote_copy(src_ref=rows_of(x, k), dst_ref=rows_of(dst, k), send_sem=i_send.at[k],
                                         recv_sem=recv.at[k], device_id={"snp": inner}, device_id_type=MESH)
            for dst, recv in ((oin, o_recv), (iin, i_recv))
        ]

    def to_outer(k):
        return remote(rows_of(iin, k), o_send.at[k], i_recv.at[k], snp=outer)

    def to_hbm(k):
        return pltpu.make_async_copy(rows_of(iin, k), rows_of(cross_hbm, k), out_sem.at[k])

    b_shift = half + (half - 1 - depth)
    heads_d = BLK // CHUNK
    dsize = HALF // heads_d

    def slot(s, carry):
        @pl.when((lax.rem(s, per) == 0) & (s < n_chunk))
        def _():
            r = pl.ds(pl.multiple_of(lax.div(s, per) * MROWS, MROWS), MROWS)
            h, l = split((dos[r] - mean[...]) * scale[...])
            dot = functools.partial(lax.dot_general, dimension_numbers=NT, preferred_element_type=jnp.float32)
            x[r] = (dot(h, high[...]) + (dot(h, low[...]) + dot(l, high[...]))) * inverse_count

        k_a = s - depth

        @pl.when((k_a >= 0) & (k_a < n_chunk))
        def _():
            plain, across_copy = to_inner(k_a)

            @pl.when(has_outer)
            def _():
                plain.wait_recv()
                r = pl.ds(pl.multiple_of(k_a * CHUNK, CHUNK), CHUNK)
                x[r] = x[r] + oin[r]

            @pl.when(middle)
            def _():
                across_copy.start()

            @pl.when(jnp.logical_not(middle))
            def _():
                plain.start()

        k_b = s - b_shift

        @pl.when((k_b >= 0) & (k_b < n_chunk))
        def _():
            to_outer(k_b).wait_recv()

            @pl.when(middle)
            def _():
                r = pl.ds(pl.multiple_of(k_b * CHUNK, CHUNK), CHUNK)
                iin[r] = x[r] + iin[r]

            @pl.when(has_outer)
            def _():
                to_outer(k_b).start()

            to_hbm(k_b).start()

            @pl.when((k_b < heads_d) & (pos == 0))
            def _():
                r = pl.ds(pl.multiple_of(k_b * CHUNK, CHUNK), CHUNK)
                diag[pl.ds(pl.multiple_of(core * BLK + k_b * CHUNK, CHUNK), CHUNK)] = iin[r]

        k_d = s - b_shift - heads_d
        ring_step(diag, dsize, dring, k_d - pos, k_d - start_b, heads_d, k_d - pos, k_d - start_b)

        @pl.when(k_d == heads_d + chips - 1)
        def _():
            for k in range(heads_d):
                sibling_wait(diag, dsize, dring, k, k)
            r = lax.broadcasted_iota(jnp.int32, (wide, wide), 0)
            c = lax.broadcasted_iota(jnp.int32, (wide, wide), 1)
            inverse[...] = diag[...] + jnp.where(r == c, 1.0, 0.0)

        k_c = k_d - (heads_d + chips)
        slab = lax.div(k_c, 2)

        @pl.when((k_c >= 0) & (slab < wide // SLAB) & (lax.rem(k_c, 2) == 0))
        def _():
            own = pl.ds(pl.multiple_of(slab * SLAB, SLAB), SLAB)
            pair = pl.ds(pl.multiple_of(lax.div(slab, 2) * 2 * SLAB, 2 * SLAB), 2 * SLAB)
            block = inverse[own, pair]
            block = jnp.where(lax.rem(slab, 2) == 0, block[:, :SLAB], block[:, SLAB:])
            r = lax.broadcasted_iota(jnp.int32, (SLAB, SLAB), 0)
            c = lax.broadcasted_iota(jnp.int32, (SLAB, SLAB), 1)
            start = jnp.concatenate([block, jnp.where(r == c, 1.0, 0.0)], 1)
            work[...] = eliminate(start, 0, SLAB // 2)

        @pl.when((k_c >= 0) & (slab < wide // SLAB) & (lax.rem(k_c, 2) == 1))
        def _():
            slab_update(slab, eliminate(work[...], SLAB // 2, SLAB), inverse, upper)

        return carry

    lax.fori_loop(0, n_chunk + 2 * half, slot, 0)
    sibling_wait(heads, HALF, ring, 0, PIECES)
    r = lax.broadcasted_iota(jnp.int32, (wide, wide), 0)
    c = lax.broadcasted_iota(jnp.int32, (wide, wide), 1)
    inverse[...] = jnp.where(r >= c, inverse[...], 0.0)
    out_d = pltpu.make_async_copy(inverse, inverse_hbm, head_sem.at[0])
    out_u = pltpu.make_async_copy(upper, upper_hbm, head_sem.at[2])
    out_u.start()
    out_h = pltpu.make_async_copy(heads, heads_hbm, head_sem.at[1])
    out_d.start()
    out_h.start()

    def finish(k, carry):
        to_inner(k)[0].wait_send()

        @pl.when(has_outer)
        def _():
            to_outer(k).wait_send()

        to_hbm(k).wait()
        return carry

    lax.fori_loop(0, n_chunk, finish, 0)

    def drain_ring(k, carry):
        drain(panels, psize, ring, k, k)
        return carry

    lax.fori_loop(0, PIECES, drain_ring, 0)
    drain(heads, HALF, ring, 0, PIECES)
    for k in range(heads_d):
        drain(diag, dsize, dring, k, k)
    for d in range(1, n_tile):
        count_copy(d).wait_send()
    out_d.wait()
    out_u.wait()
    out_h.wait()


def gather_cross(dosages, phenotypes, n_tile, n_snp):
    rows, snps = dosages.shape
    wide = 2 * BLK
    f32 = jnp.float32
    n_chunk = rows // CHUNK
    dma = pltpu.SemaphoreType.DMA
    return pl.pallas_call(
        functools.partial(kernel, n_tile, n_snp),
        out_shape=(
            jax.ShapeDtypeStruct((rows, wide), f32),
            jax.ShapeDtypeStruct((wide, wide), f32),
            jax.ShapeDtypeStruct((wide, wide), f32),
            jax.ShapeDtypeStruct((wide, phenotypes.shape[1]), f32),
        ),
        in_specs=[pl.BlockSpec(memory_space=pl.ANY)] * 2,
        out_specs=[pl.BlockSpec(memory_space=pl.ANY)] * 4,
        scratch_shapes=[
            pltpu.VMEM((rows, snps), f32),
            pltpu.VMEM((wide, snps), f32),
            pltpu.VMEM((wide, phenotypes.shape[1]), f32),
            pltpu.VMEM((wide, wide), f32),
            pltpu.VMEM((wide, wide), f32),
            pltpu.VMEM((wide, wide), f32),
            pltpu.VMEM((SLAB, 2 * SLAB), f32),
            pltpu.VMEM((wide, snps), jnp.bfloat16),
            pltpu.VMEM((wide, snps), jnp.bfloat16),
            pltpu.VMEM((n_tile, 1, snps), f32),
            pltpu.VMEM((1, snps), f32),
            pltpu.VMEM((1, snps), f32),
            pltpu.VMEM((rows, wide), f32),
            pltpu.VMEM((rows, wide), f32),
            pltpu.VMEM((rows, wide), f32),
            dma((rows // MROWS,)),
            dma((3,)),
            dma((n_chunk,)),
            dma((n_tile,)),
            dma((n_tile,)),
        ]
        + [dma((PIECES + 1,))] * 8
        + [dma((BLK // CHUNK,))] * 8
        + [dma((n_chunk,))] * 4,
        compiler_params=pltpu.CompilerParams(
            collective_id=0, has_side_effects=True, vmem_limit_bytes=58 * 1024 * 1024
        ),
    )(dosages, phenotypes)


def body(dosages, phenotypes):
    n_tile = lax.axis_size("tile")
    n_snp = lax.axis_size("snp")
    tile_index = lax.axis_index("tile")
    cross, inverse, upper, heads = gather_cross(dosages, phenotypes, n_tile, n_snp)
    exact = functools.partial(lax.dot_general, precision=lax.Precision.HIGHEST, preferred_element_type=jnp.float32)
    factor = exact(cross, inverse, NT)
    lower = upper.T
    solved = jnp.dot(inverse, heads, precision=lax.Precision.HIGHEST)
    head_rows = jnp.where(
        tile_index == 0, lower[:BLK], jnp.where(tile_index == 1, lower[BLK:], factor[:BLK])
    )
    factor = factor.at[:BLK].set(head_rows)
    current = phenotypes - jnp.dot(factor, solved, precision=lax.Precision.HIGHEST)
    head = jnp.where(tile_index == 0, solved[:BLK], jnp.where(tile_index == 1, solved[BLK:], current[:BLK]))
    return (factor, current.at[:BLK].set(head))


def solution(mesh):
    placed = (P("tile", "snp"), P("tile", "snp"))
    return jax.shard_map(
        body,
        mesh=mesh,
        in_specs=placed,
        out_specs=(P("tile", None), P("tile", "snp")),
        check_vma=False,
    )
```

```python
import functools

import jax
import jax.numpy as jnp
from jax import lax
from jax.experimental import pallas as pl
from jax.experimental.pallas import tpu as pltpu
from jax.sharding import PartitionSpec as P

BLK = 256
HALF = BLK // 2
PIECES = 16
GROUPS = 4
HOP = 2
DIAG_PIECES = 4
MROWS = 256
SLAB = 64
MESH = pl.DeviceIdType.MESH
NT = (((1,), (1,)), ((), ()))


def split(value):
    high = value.astype(jnp.bfloat16)
    return high, (value - high.astype(jnp.float32)).astype(jnp.bfloat16)


def eliminate(work, first, last):
    below = lax.broadcasted_iota(jnp.int32, (SLAB, 1), 0)
    for j in range(first, last):
        column = jnp.where(below > j, work[:, j:j + 1], 0.0)
        work = work - column * (work[j:j + 1] * (1.0 / work[j:j + 1, j:j + 1]))
    return work


def slab_update(b, work, inverse, upper):
    wide = inverse.shape[0]
    exact = functools.partial(jnp.dot, precision=lax.Precision.HIGHEST, preferred_element_type=jnp.float32)
    r = lax.broadcasted_iota(jnp.int32, work.shape, 0)
    c = lax.broadcasted_iota(jnp.int32, work.shape, 1)
    pivots = jnp.sum(jnp.where(r == c, work, 0.0), axis=1, keepdims=True)
    work = work * lax.rsqrt(pivots)
    own = pl.ds(pl.multiple_of(b * SLAB, SLAB), SLAB)
    lane = lax.broadcasted_iota(jnp.int32, (SLAB, wide), 1)
    mine = (lane >= b * SLAB) & (lane < (b + 1) * SLAB)
    after = lane >= (b + 1) * SLAB
    upper_block = jnp.where(c < SLAB, jnp.where(c >= r, work, 0.0), 0.0)[:, :SLAB]
    inverse_block = work[:, SLAB:]
    repeat = wide // SLAB
    solved = exact(inverse_block, inverse[own])
    solved = jnp.where(mine, jnp.concatenate([inverse_block] * repeat, 1), solved)
    later = jnp.where(after, solved, 0.0)
    upper[own] = jnp.where(mine, jnp.concatenate([upper_block] * repeat, 1), later)
    inverse[own] = solved
    row_all = lax.broadcasted_iota(jnp.int32, (wide, wide), 0)
    lane_all = lax.broadcasted_iota(jnp.int32, (wide, wide), 1)
    cleared = (row_all >= (b + 1) * SLAB) & (lane_all >= b * SLAB) & (lane_all < (b + 1) * SLAB)
    inverse[...] = jnp.where(cleared, 0.0, inverse[...]) - exact(later.T, solved)


def kernel(n_tile, n_snp, dos_hbm, phe_hbm, cross_hbm, inverse_hbm, upper_hbm, heads_hbm,
           dos, panels, heads, diag, inverse, upper, work, high, low, counts, mean, scale, x, oin, iin,
           load_sem, head_sem, out_sem, cnt_send, cnt_recv,
           a_send, a_recv, b_send, b_recv, sa_send, sa_recv, sb_send, sb_recv,
           da_send, da_recv, db_send, db_recv, ea_send, ea_recv, eb_send, eb_recv,
           i_send, o_recv, o_send, i_recv):
    rows, snps = dos.shape
    wide = 2 * BLK
    tile = lax.axis_index("tile")
    snp = lax.axis_index("snp")
    chips = n_tile // 2
    across = chips // 2
    core = lax.rem(tile, 2)
    chip = lax.div(tile, 2)
    pos = jnp.where(chip < across, chip, chips + across - 1 - chip)
    sib = chip * 2 + 1 - core

    def at_pos(q):
        q = lax.rem(q + chips, chips)
        return 2 * jnp.where(q < across, q, chips + across - 1 - q) + core

    right, left = at_pos(pos + 1), at_pos(pos - 1)
    half = n_snp // 2
    lower = snp < half
    depth = jnp.where(lower, snp, n_snp - 1 - snp)
    inner = jnp.where(lower, snp + 1, snp - 1)
    outer = jnp.where(lower, snp - 1, snp + 1)
    middle = depth == half - 1
    has_outer = depth > 0

    barrier = pltpu.get_barrier_semaphore()
    for d in range(1, n_tile):
        pl.semaphore_signal(barrier, inc=1, device_id={"tile": lax.rem(tile + d, n_tile)}, device_id_type=MESH)
    pl.semaphore_signal(barrier, inc=1, device_id={"snp": inner}, device_id_type=MESH)

    @pl.when(has_outer)
    def _():
        pl.semaphore_signal(barrier, inc=1, device_id={"snp": outer}, device_id_type=MESH)

    def load(k):
        r = pl.ds(pl.multiple_of(k * MROWS, MROWS), MROWS)
        return pltpu.make_async_copy(dos_hbm.at[r], dos.at[r], load_sem.at[k])

    n_load = rows // MROWS
    own = pl.ds(pl.multiple_of(core * BLK, BLK), BLK)
    own_panel = pltpu.make_async_copy(dos_hbm.at[pl.ds(0, BLK)], panels.at[own], head_sem.at[0])
    own_heads = pltpu.make_async_copy(phe_hbm.at[pl.ds(0, BLK)], heads.at[own], head_sem.at[1])

    @pl.when(pos == 0)
    def _():
        own_panel.start()
        own_heads.start()

    for k in range(n_load):
        load(k).start()
    pl.semaphore_wait(barrier, n_tile + jnp.where(has_outer, 1, 0))

    @pl.when(pos == 0)
    def _():
        own_panel.wait()
        own_heads.wait()

    def remote(ref, send, recv, **where):
        return pltpu.make_async_remote_copy(src_ref=ref, dst_ref=ref, send_sem=send, recv_sem=recv,
                                            device_id=where, device_id_type=MESH)

    def piece(buf, which, side, k, size):
        return buf.at[pl.ds(pl.multiple_of(which * BLK + (2 * k + side) * size, size), size)]

    def ring_step(buf, size, sems, k_a, k_b, last, index_a, index_b):
        (asn, arc, bsn, brc, sas, sar, sbs, sbr) = sems

        @pl.when((k_a >= 0) & (k_a < last))
        def _():
            ref = piece(buf, core, 0, k_a, size)
            i = index_a
            d = remote(ref, asn.at[i], arc.at[i], tile=right)

            @pl.when(pos > 0)
            def _():
                d.wait_recv()

            @pl.when(pos < chips - 1)
            def _():
                d.start()

            remote(ref, sas.at[i], sar.at[i], tile=sib).start()

        @pl.when((k_b >= 0) & (k_b < last))
        def _():
            ref = piece(buf, core, 1, k_b, size)
            i = index_b
            d = remote(ref, bsn.at[i], brc.at[i], tile=left)

            @pl.when(pos > 0)
            def _():
                d.wait_recv()

            @pl.when(pos != 1)
            def _():
                d.start()

            remote(ref, sbs.at[i], sbr.at[i], tile=sib).start()

    def sibling_wait(buf, size, sems, k, i):
        (asn, arc, bsn, brc, sas, sar, sbs, sbr) = sems
        remote(piece(buf, 1 - core, 0, k, size), sas.at[i], sar.at[i], tile=sib).wait_recv()
        remote(piece(buf, 1 - core, 1, k, size), sbs.at[i], sbr.at[i], tile=sib).wait_recv()

    def drain(buf, size, sems, k, i):
        (asn, arc, bsn, brc, sas, sar, sbs, sbr) = sems
        ref_a, ref_b = piece(buf, core, 0, k, size), piece(buf, core, 1, k, size)

        @pl.when(pos < chips - 1)
        def _():
            remote(ref_a, asn.at[i], arc.at[i], tile=right).wait_send()

        @pl.when(pos != 1)
        def _():
            remote(ref_b, bsn.at[i], brc.at[i], tile=left).wait_send()

        remote(ref_a, sas.at[i], sar.at[i], tile=sib).wait_send()
        remote(ref_b, sbs.at[i], sbr.at[i], tile=sib).wait_send()

    ring = (a_send, a_recv, b_send, b_recv, sa_send, sa_recv, sb_send, sb_recv)
    dring = (da_send, da_recv, db_send, db_recv, ea_send, ea_recv, eb_send, eb_recv)
    psize = HALF // PIECES
    start_b = lax.rem(chips - pos, chips)

    def count_copy(d):
        ref = counts.at[tile]
        return remote(ref, cnt_send.at[d], cnt_recv.at[tile], tile=lax.rem(tile + d, n_tile))

    def ring_slot(s, total):
        @pl.when(s < n_load)
        def _():
            load(s).wait()
        r = jnp.minimum(s, n_load - 1)
        part = jnp.sum(dos[pl.ds(pl.multiple_of(r * MROWS, MROWS), MROWS)].reshape(MROWS // 8, 8, snps), axis=0)
        total = total + jnp.where(s < n_load, part, 0.0)
        ring_step(panels, psize, ring, s - pos, s - start_b, PIECES, s - pos, s - start_b)
        return total

    first = max(n_load, PIECES // GROUPS + chips)
    total = lax.fori_loop(0, n_load, ring_slot, jnp.zeros((8, snps), jnp.float32))
    counts[tile] = jnp.sum(total, axis=0, keepdims=True)
    for d in range(1, n_tile):
        count_copy(d).start()

    def ring_rest(s, carry):
        ring_step(panels, psize, ring, s - pos, s - start_b, PIECES, s - pos, s - start_b)
        return carry

    lax.fori_loop(n_load, first, ring_rest, 0)
    for d in range(1, n_tile):
        source = lax.rem(tile + d, n_tile)
        remote(counts.at[source], cnt_send.at[d], cnt_recv.at[source], tile=source).wait_recv()
    freq = counts[0]
    for t in range(1, n_tile):
        freq = freq + counts[t]
    freq = freq / (2.0 * rows * n_tile)
    mean[...] = 2.0 * freq
    scale[...] = lax.rsqrt(jnp.maximum(2.0 * freq * (1.0 - freq), 0.05))

    def wait_sib(k, carry):
        sibling_wait(panels, psize, ring, k, k)
        return carry

    gsize = BLK // GROUPS

    def standardize(g, carry):
        for p in range(2):
            source = pl.ds(pl.multiple_of(p * BLK + g * gsize, gsize), gsize)
            target = pl.ds(pl.multiple_of((2 * g + p) * gsize, gsize), gsize)
            h, l = split((panels[source] - mean[...]) * scale[...])
            high[target] = h
            low[target] = l
        return carry

    lax.fori_loop(0, PIECES // GROUPS, wait_sib, 0)
    standardize(0, 0)

    per = rows // MROWS
    n_chunk = per * GROUPS
    lanes = wide // GROUPS
    inverse_count = 1.0 / (snps * n_snp)

    def rows_of(buf, k):
        return buf.at[pl.ds(pl.multiple_of(k * MROWS, MROWS), MROWS)]

    def place(k):
        late = jnp.maximum(k - (per + GROUPS - 1), 0)
        early = k < per + GROUPS - 1
        group = jnp.where(k < per, 0, jnp.where(early, k - per + 1, 1 + lax.div(late, per - 1)))
        block = jnp.where(k < per, k, jnp.where(early, 0, 1 + lax.rem(late, per - 1)))
        return group, block

    def to_inner(k):
        return [
            pltpu.make_async_remote_copy(src_ref=rows_of(x, k), dst_ref=rows_of(dst, k), send_sem=i_send.at[k],
                                         recv_sem=recv.at[k], device_id={"snp": inner}, device_id_type=MESH)
            for dst, recv in ((oin, o_recv), (iin, i_recv))
        ]

    def to_outer(k):
        return remote(rows_of(iin, k), o_send.at[k], i_recv.at[k], snp=outer)

    def to_hbm(k):
        group, block = place(k)
        r = pl.ds(pl.multiple_of(block * MROWS, MROWS), MROWS)
        c = pl.ds(pl.multiple_of(group * lanes, lanes), lanes)
        return pltpu.make_async_copy(rows_of(iin, k), cross_hbm.at[r, c], out_sem.at[k])

    b_shift = HOP * (half + (half - 1 - depth))
    heads_d = DIAG_PIECES
    dsize = HALF // heads_d
    ready = per + GROUPS - 2

    def slot(s, carry):
        for i in range(2):
            k_r = first + 2 * s + i
            ring_step(panels, psize, ring, k_r - pos, k_r - start_b, PIECES, k_r - pos, k_r - start_b)

        @pl.when(s == per - 1)
        def _():
            ring_step(heads, HALF, ring, 0, jnp.where(pos == 0, 0, -1), 1, PIECES, PIECES)

            @pl.when(pos > 0)
            def _():
                ring_step(heads, HALF, ring, -1, 0, 1, PIECES, PIECES)

            lax.fori_loop(PIECES // GROUPS, PIECES, wait_sib, 0)
            lax.fori_loop(1, GROUPS, standardize, 0)

        @pl.when(s < n_chunk)
        def _():
            group, block = place(s)
            r = pl.ds(pl.multiple_of(block * MROWS, MROWS), MROWS)
            g = pl.ds(pl.multiple_of(group * lanes, lanes), lanes)
            h, l = split((dos[r] - mean[...]) * scale[...])
            dot = functools.partial(lax.dot_general, dimension_numbers=NT, preferred_element_type=jnp.float32)
            value = dot(h, high[g]) + (dot(h, low[g]) + dot(l, high[g]))
            x[pl.ds(pl.multiple_of(s * MROWS, MROWS), MROWS)] = value * inverse_count

        k_a = s - HOP * depth

        @pl.when((k_a >= 0) & (k_a < n_chunk))
        def _():
            plain, across_copy = to_inner(k_a)

            @pl.when(has_outer)
            def _():
                plain.wait_recv()
                r = pl.ds(pl.multiple_of(k_a * MROWS, MROWS), MROWS)
                x[r] = x[r] + oin[r]

            @pl.when(middle)
            def _():
                across_copy.start()

            @pl.when(jnp.logical_not(middle))
            def _():
                plain.start()

        k_b = s - b_shift

        @pl.when((k_b >= 0) & (k_b < n_chunk))
        def _():
            to_outer(k_b).wait_recv()

            @pl.when(middle)
            def _():
                r = pl.ds(pl.multiple_of(k_b * MROWS, MROWS), MROWS)
                iin[r] = x[r] + iin[r]

            @pl.when(has_outer)
            def _():
                to_outer(k_b).start()

            to_hbm(k_b).start()

        @pl.when(k_b == ready)
        def _():
            @pl.when(pos == 0)
            def _():
                parts = [iin[k * MROWS:(k + 1) * MROWS] for k in (0, *range(per, per + GROUPS - 1))]
                diag[own] = jnp.concatenate([p[:, :gsize] for p in parts] + [p[:, gsize:] for p in parts], 1)

            def diag_slot(k_d, carry):
                ring_step(diag, dsize, dring, k_d - pos, k_d - start_b, heads_d, k_d - pos, k_d - start_b)
                return carry

            lax.fori_loop(0, heads_d + chips - 1, diag_slot, 0)
            for k in range(heads_d):
                sibling_wait(diag, dsize, dring, k, k)
            r = lax.broadcasted_iota(jnp.int32, (wide, wide), 0)
            c = lax.broadcasted_iota(jnp.int32, (wide, wide), 1)
            inverse[...] = diag[...] + jnp.where(r == c, 1.0, 0.0)

        k_c = k_b - ready - 1
        slab = lax.div(k_c, 2)

        @pl.when((k_c >= 0) & (slab < wide // SLAB) & (lax.rem(k_c, 2) == 0))
        def _():
            mine = pl.ds(pl.multiple_of(slab * SLAB, SLAB), SLAB)
            pair = pl.ds(pl.multiple_of(lax.div(slab, 2) * 2 * SLAB, 2 * SLAB), 2 * SLAB)
            block = inverse[mine, pair]
            block = jnp.where(lax.rem(slab, 2) == 0, block[:, :SLAB], block[:, SLAB:])
            r = lax.broadcasted_iota(jnp.int32, (SLAB, SLAB), 0)
            c = lax.broadcasted_iota(jnp.int32, (SLAB, SLAB), 1)
            start = jnp.concatenate([block, jnp.where(r == c, 1.0, 0.0)], 1)
            work[...] = eliminate(start, 0, SLAB // 2)

        @pl.when((k_c >= 0) & (slab < wide // SLAB) & (lax.rem(k_c, 2) == 1))
        def _():
            slab_update(slab, eliminate(work[...], SLAB // 2, SLAB), inverse, upper)

        return carry

    lax.fori_loop(0, n_chunk + HOP * (n_snp - 1) + 1, slot, 0)
    sibling_wait(heads, HALF, ring, 0, PIECES)
    r = lax.broadcasted_iota(jnp.int32, (wide, wide), 0)
    c = lax.broadcasted_iota(jnp.int32, (wide, wide), 1)
    inverse[...] = jnp.where(r >= c, inverse[...], 0.0)
    out_d = pltpu.make_async_copy(inverse, inverse_hbm, head_sem.at[0])
    out_u = pltpu.make_async_copy(upper, upper_hbm, head_sem.at[2])
    out_u.start()
    out_h = pltpu.make_async_copy(heads, heads_hbm, head_sem.at[1])
    out_d.start()
    out_h.start()

    def finish(k, carry):
        to_inner(k)[0].wait_send()

        @pl.when(has_outer)
        def _():
            to_outer(k).wait_send()

        to_hbm(k).wait()
        return carry

    lax.fori_loop(0, n_chunk, finish, 0)

    def drain_ring(k, carry):
        drain(panels, psize, ring, k, k)
        return carry

    lax.fori_loop(0, PIECES, drain_ring, 0)
    drain(heads, HALF, ring, 0, PIECES)
    for k in range(heads_d):
        drain(diag, dsize, dring, k, k)
    for d in range(1, n_tile):
        count_copy(d).wait_send()
    out_d.wait()
    out_u.wait()
    out_h.wait()


def gather_cross(dosages, phenotypes, n_tile, n_snp):
    rows, snps = dosages.shape
    wide = 2 * BLK
    f32 = jnp.float32
    n_chunk = rows // MROWS * GROUPS
    lanes = wide // GROUPS
    dma = pltpu.SemaphoreType.DMA
    return pl.pallas_call(
        functools.partial(kernel, n_tile, n_snp),
        out_shape=(
            jax.ShapeDtypeStruct((rows, wide), f32),
            jax.ShapeDtypeStruct((wide, wide), f32),
            jax.ShapeDtypeStruct((wide, wide), f32),
            jax.ShapeDtypeStruct((wide, phenotypes.shape[1]), f32),
        ),
        in_specs=[pl.BlockSpec(memory_space=pl.ANY)] * 2,
        out_specs=[pl.BlockSpec(memory_space=pl.ANY)] * 4,
        scratch_shapes=[
            pltpu.VMEM((rows, snps), f32),
            pltpu.VMEM((wide, snps), f32),
            pltpu.VMEM((wide, phenotypes.shape[1]), f32),
            pltpu.VMEM((wide, wide), f32),
            pltpu.VMEM((wide, wide), f32),
            pltpu.VMEM((wide, wide), f32),
            pltpu.VMEM((SLAB, 2 * SLAB), f32),
            pltpu.VMEM((wide, snps), jnp.bfloat16),
            pltpu.VMEM((wide, snps), jnp.bfloat16),
            pltpu.VMEM((n_tile, 1, snps), f32),
            pltpu.VMEM((1, snps), f32),
            pltpu.VMEM((1, snps), f32),
            pltpu.VMEM((rows * GROUPS, lanes), f32),
            pltpu.VMEM((rows * GROUPS, lanes), f32),
            pltpu.VMEM((rows * GROUPS, lanes), f32),
            dma((rows // MROWS,)),
            dma((3,)),
            dma((n_chunk,)),
            dma((n_tile,)),
            dma((n_tile,)),
        ]
        + [dma((PIECES + 1,))] * 8
        + [dma((DIAG_PIECES,))] * 8
        + [dma((n_chunk,))] * 4,
        compiler_params=pltpu.CompilerParams(
            collective_id=0, has_side_effects=True, vmem_limit_bytes=58 * 1024 * 1024
        ),
    )(dosages, phenotypes)


def body(dosages, phenotypes):
    n_tile = lax.axis_size("tile")
    n_snp = lax.axis_size("snp")
    tile_index = lax.axis_index("tile")
    cross, inverse, upper, heads = gather_cross(dosages, phenotypes, n_tile, n_snp)
    exact = functools.partial(lax.dot_general, precision=lax.Precision.HIGHEST, preferred_element_type=jnp.float32)
    wide = 2 * BLK
    ordered = inverse.reshape(wide, 2, GROUPS, BLK // GROUPS).transpose(0, 2, 1, 3).reshape(wide, wide)
    factor = exact(cross, ordered, NT)
    lower = upper.T
    solved = jnp.dot(inverse, heads, precision=lax.Precision.HIGHEST)
    head_rows = jnp.where(
        tile_index == 0, lower[:BLK], jnp.where(tile_index == 1, lower[BLK:], factor[:BLK])
    )
    factor = factor.at[:BLK].set(head_rows)
    current = phenotypes - jnp.dot(factor, solved, precision=lax.Precision.HIGHEST)
    head = jnp.where(tile_index == 0, solved[:BLK], jnp.where(tile_index == 1, solved[BLK:], current[:BLK]))
    return (factor, current.at[:BLK].set(head))


def solution(mesh):
    placed = (P("tile", "snp"), P("tile", "snp"))
    return jax.shard_map(
        body,
        mesh=mesh,
        in_specs=placed,
        out_specs=(P("tile", None), P("tile", "snp")),
        check_vma=False,
    )
```

```python
import functools

import jax
import jax.numpy as jnp
from jax import lax
from jax.experimental import pallas as pl
from jax.experimental.pallas import tpu as pltpu
from jax.sharding import PartitionSpec as P

BLK = 256
HALF = BLK // 2
PIECES = 16
GROUPS = 4
HOP = 2
PACE = 3
DIAG_PIECES = 4
MROWS = 256
SLAB = 64
MESH = pl.DeviceIdType.MESH
NT = (((1,), (1,)), ((), ()))


def split(value):
    high = value.astype(jnp.bfloat16)
    return high, (value - high.astype(jnp.float32)).astype(jnp.bfloat16)


def eliminate(work, first, last):
    below = lax.broadcasted_iota(jnp.int32, (SLAB, 1), 0)
    for j in range(first, last):
        column = jnp.where(below > j, work[:, j:j + 1], 0.0)
        work = work - column * (work[j:j + 1] * (1.0 / work[j:j + 1, j:j + 1]))
    return work


def slab_update(b, work, inverse, upper):
    wide = inverse.shape[0]
    exact = functools.partial(jnp.dot, precision=lax.Precision.HIGHEST, preferred_element_type=jnp.float32)
    r = lax.broadcasted_iota(jnp.int32, work.shape, 0)
    c = lax.broadcasted_iota(jnp.int32, work.shape, 1)
    pivots = jnp.sum(jnp.where(r == c, work, 0.0), axis=1, keepdims=True)
    work = work * lax.rsqrt(pivots)
    own = pl.ds(pl.multiple_of(b * SLAB, SLAB), SLAB)
    lane = lax.broadcasted_iota(jnp.int32, (SLAB, wide), 1)
    mine = (lane >= b * SLAB) & (lane < (b + 1) * SLAB)
    after = lane >= (b + 1) * SLAB
    upper_block = jnp.where(c < SLAB, jnp.where(c >= r, work, 0.0), 0.0)[:, :SLAB]
    inverse_block = work[:, SLAB:]
    repeat = wide // SLAB
    solved = exact(inverse_block, inverse[own])
    solved = jnp.where(mine, jnp.concatenate([inverse_block] * repeat, 1), solved)
    later = jnp.where(after, solved, 0.0)
    upper[own] = jnp.where(mine, jnp.concatenate([upper_block] * repeat, 1), later)
    inverse[own] = solved
    row_all = lax.broadcasted_iota(jnp.int32, (wide, wide), 0)
    lane_all = lax.broadcasted_iota(jnp.int32, (wide, wide), 1)
    cleared = (row_all >= (b + 1) * SLAB) & (lane_all >= b * SLAB) & (lane_all < (b + 1) * SLAB)
    inverse[...] = jnp.where(cleared, 0.0, inverse[...]) - exact(later.T, solved)


def kernel(n_tile, n_snp, dos_hbm, phe_hbm, cross_hbm, inverse_hbm, upper_hbm, heads_hbm,
           dos, panels, heads, diag, inverse, upper, work, high, low, counts, mean, scale, x, oin, iin,
           load_sem, head_sem, out_sem, cnt_send, cnt_recv,
           a_send, a_recv, b_send, b_recv, sa_send, sa_recv, sb_send, sb_recv,
           da_send, da_recv, db_send, db_recv, ea_send, ea_recv, eb_send, eb_recv,
           i_send, o_recv, o_send, i_recv):
    rows, snps = dos.shape
    wide = 2 * BLK
    tile = lax.axis_index("tile")
    snp = lax.axis_index("snp")
    chips = n_tile // 2
    across = chips // 2
    core = lax.rem(tile, 2)
    chip = lax.div(tile, 2)
    pos = jnp.where(chip < across, chip, chips + across - 1 - chip)
    sib = chip * 2 + 1 - core

    def at_pos(q):
        q = lax.rem(q + chips, chips)
        return 2 * jnp.where(q < across, q, chips + across - 1 - q) + core

    right, left = at_pos(pos + 1), at_pos(pos - 1)
    half = n_snp // 2
    lower = snp < half
    depth = jnp.where(lower, snp, n_snp - 1 - snp)
    inner = jnp.where(lower, snp + 1, snp - 1)
    outer = jnp.where(lower, snp - 1, snp + 1)
    middle = depth == half - 1
    has_outer = depth > 0

    barrier = pltpu.get_barrier_semaphore()
    for d in range(1, n_tile):
        pl.semaphore_signal(barrier, inc=1, device_id={"tile": lax.rem(tile + d, n_tile)}, device_id_type=MESH)
    pl.semaphore_signal(barrier, inc=1, device_id={"snp": inner}, device_id_type=MESH)

    @pl.when(has_outer)
    def _():
        pl.semaphore_signal(barrier, inc=1, device_id={"snp": outer}, device_id_type=MESH)

    def load(k):
        r = pl.ds(pl.multiple_of(k * MROWS, MROWS), MROWS)
        return pltpu.make_async_copy(dos_hbm.at[r], dos.at[r], load_sem.at[k])

    n_load = rows // MROWS
    own = pl.ds(pl.multiple_of(core * BLK, BLK), BLK)
    own_panel = pltpu.make_async_copy(dos_hbm.at[pl.ds(0, BLK)], panels.at[own], head_sem.at[0])
    own_heads = pltpu.make_async_copy(phe_hbm.at[pl.ds(0, BLK)], heads.at[own], head_sem.at[1])

    @pl.when(pos == 0)
    def _():
        own_panel.start()
        own_heads.start()

    for k in range(n_load):
        load(k).start()
    pl.semaphore_wait(barrier, n_tile + jnp.where(has_outer, 1, 0))

    @pl.when(pos == 0)
    def _():
        own_panel.wait()
        own_heads.wait()

    def remote(ref, send, recv, **where):
        return pltpu.make_async_remote_copy(src_ref=ref, dst_ref=ref, send_sem=send, recv_sem=recv,
                                            device_id=where, device_id_type=MESH)

    def piece(buf, which, side, k, size):
        return buf.at[pl.ds(pl.multiple_of(which * BLK + (2 * k + side) * size, size), size)]

    def ring_step(buf, size, sems, k_a, k_b, last, index_a, index_b, paced=False):
        (asn, arc, bsn, brc, sas, sar, sbs, sbr) = sems

        @pl.when((k_a >= 0) & (k_a < last))
        def _():
            ref = piece(buf, core, 0, k_a, size)
            i = index_a
            d = remote(ref, asn.at[i], arc.at[i], tile=right)

            @pl.when(pos > 0)
            def _():
                d.wait_recv()

            if paced:
                @pl.when((pos == 0) & (k_a >= PACE))
                def _():
                    j = jnp.maximum(k_a - PACE, 0)
                    remote(piece(buf, core, 0, j, size), asn.at[j], arc.at[j], tile=right).wait_send()

            @pl.when(pos < chips - 1)
            def _():
                d.start()

            remote(ref, sas.at[i], sar.at[i], tile=sib).start()

        @pl.when((k_b >= 0) & (k_b < last))
        def _():
            ref = piece(buf, core, 1, k_b, size)
            i = index_b
            d = remote(ref, bsn.at[i], brc.at[i], tile=left)

            @pl.when(pos > 0)
            def _():
                d.wait_recv()

            if paced:
                @pl.when((pos == 0) & (k_b >= PACE))
                def _():
                    j = jnp.maximum(k_b - PACE, 0)
                    remote(piece(buf, core, 1, j, size), bsn.at[j], brc.at[j], tile=left).wait_send()

            @pl.when(pos != 1)
            def _():
                d.start()

            remote(ref, sbs.at[i], sbr.at[i], tile=sib).start()

    def sibling_wait(buf, size, sems, k, i):
        (asn, arc, bsn, brc, sas, sar, sbs, sbr) = sems
        remote(piece(buf, 1 - core, 0, k, size), sas.at[i], sar.at[i], tile=sib).wait_recv()
        remote(piece(buf, 1 - core, 1, k, size), sbs.at[i], sbr.at[i], tile=sib).wait_recv()

    def drain(buf, size, sems, k, i, waiting=True):
        (asn, arc, bsn, brc, sas, sar, sbs, sbr) = sems
        ref_a, ref_b = piece(buf, core, 0, k, size), piece(buf, core, 1, k, size)

        @pl.when((pos < chips - 1) & waiting)
        def _():
            remote(ref_a, asn.at[i], arc.at[i], tile=right).wait_send()

        @pl.when((pos != 1) & waiting)
        def _():
            remote(ref_b, bsn.at[i], brc.at[i], tile=left).wait_send()

        remote(ref_a, sas.at[i], sar.at[i], tile=sib).wait_send()
        remote(ref_b, sbs.at[i], sbr.at[i], tile=sib).wait_send()

    ring = (a_send, a_recv, b_send, b_recv, sa_send, sa_recv, sb_send, sb_recv)
    dring = (da_send, da_recv, db_send, db_recv, ea_send, ea_recv, eb_send, eb_recv)
    psize = HALF // PIECES
    start_b = lax.rem(chips - pos, chips)

    def count_copy(d):
        ref = counts.at[tile]
        return remote(ref, cnt_send.at[d], cnt_recv.at[tile], tile=lax.rem(tile + d, n_tile))

    def ring_slot(s, total):
        @pl.when(s < n_load)
        def _():
            load(s).wait()
        r = jnp.minimum(s, n_load - 1)
        part = jnp.sum(dos[pl.ds(pl.multiple_of(r * MROWS, MROWS), MROWS)].reshape(MROWS // 8, 8, snps), axis=0)
        total = total + jnp.where(s < n_load, part, 0.0)
        ring_step(panels, psize, ring, s - pos, s - start_b, PIECES, s - pos, s - start_b, paced=True)
        return total

    first = max(n_load, PIECES // GROUPS + chips)
    total = lax.fori_loop(0, n_load, ring_slot, jnp.zeros((8, snps), jnp.float32))
    counts[tile] = jnp.sum(total, axis=0, keepdims=True)
    for d in range(1, n_tile):
        count_copy(d).start()

    def ring_rest(s, carry):
        ring_step(panels, psize, ring, s - pos, s - start_b, PIECES, s - pos, s - start_b, paced=True)
        return carry

    lax.fori_loop(n_load, first, ring_rest, 0)
    for d in range(1, n_tile):
        source = lax.rem(tile + d, n_tile)
        remote(counts.at[source], cnt_send.at[d], cnt_recv.at[source], tile=source).wait_recv()
    freq = counts[0]
    for t in range(1, n_tile):
        freq = freq + counts[t]
    freq = freq / (2.0 * rows * n_tile)
    mean[...] = 2.0 * freq
    scale[...] = lax.rsqrt(jnp.maximum(2.0 * freq * (1.0 - freq), 0.05))

    def wait_sib(k, carry):
        sibling_wait(panels, psize, ring, k, k)
        return carry

    gsize = BLK // GROUPS

    def standardize(g, carry):
        for p in range(2):
            source = pl.ds(pl.multiple_of(p * BLK + g * gsize, gsize), gsize)
            target = pl.ds(pl.multiple_of((2 * g + p) * gsize, gsize), gsize)
            h, l = split((panels[source] - mean[...]) * scale[...])
            high[target] = h
            low[target] = l
        return carry

    lax.fori_loop(0, PIECES // GROUPS, wait_sib, 0)
    standardize(0, 0)

    per = rows // MROWS
    n_chunk = per * GROUPS
    lanes = wide // GROUPS
    inverse_count = 1.0 / (snps * n_snp)

    def rows_of(buf, k):
        return buf.at[pl.ds(pl.multiple_of(k * MROWS, MROWS), MROWS)]

    def place(k):
        late = jnp.maximum(k - (per + GROUPS - 1), 0)
        early = k < per + GROUPS - 1
        group = jnp.where(k < per, 0, jnp.where(early, k - per + 1, 1 + lax.div(late, per - 1)))
        block = jnp.where(k < per, k, jnp.where(early, 0, 1 + lax.rem(late, per - 1)))
        return group, block

    def to_inner(k):
        return [
            pltpu.make_async_remote_copy(src_ref=rows_of(x, k), dst_ref=rows_of(dst, k), send_sem=i_send.at[k],
                                         recv_sem=recv.at[k], device_id={"snp": inner}, device_id_type=MESH)
            for dst, recv in ((oin, o_recv), (iin, i_recv))
        ]

    def to_outer(k):
        return remote(rows_of(iin, k), o_send.at[k], i_recv.at[k], snp=outer)

    def to_hbm(k):
        group, block = place(k)
        r = pl.ds(pl.multiple_of(block * MROWS, MROWS), MROWS)
        c = pl.ds(pl.multiple_of(group * lanes, lanes), lanes)
        return pltpu.make_async_copy(rows_of(iin, k), cross_hbm.at[r, c], out_sem.at[k])

    b_shift = HOP * (half + (half - 1 - depth))
    heads_d = DIAG_PIECES
    dsize = HALF // heads_d
    ready = per + GROUPS - 2

    def slot(s, carry):
        for i in range(2):
            k_r = first + 2 * s + i
            ring_step(panels, psize, ring, k_r - pos, k_r - start_b, PIECES, k_r - pos, k_r - start_b, paced=True)

        @pl.when(s == per - 1)
        def _():
            ring_step(heads, HALF, ring, 0, jnp.where(pos == 0, 0, -1), 1, PIECES, PIECES)

            @pl.when(pos > 0)
            def _():
                ring_step(heads, HALF, ring, -1, 0, 1, PIECES, PIECES)

            lax.fori_loop(PIECES // GROUPS, PIECES, wait_sib, 0)
            lax.fori_loop(1, GROUPS, standardize, 0)

        @pl.when(s < n_chunk)
        def _():
            group, block = place(s)
            r = pl.ds(pl.multiple_of(block * MROWS, MROWS), MROWS)
            g = pl.ds(pl.multiple_of(group * lanes, lanes), lanes)
            h, l = split((dos[r] - mean[...]) * scale[...])
            dot = functools.partial(lax.dot_general, dimension_numbers=NT, preferred_element_type=jnp.float32)
            value = dot(h, high[g]) + (dot(h, low[g]) + dot(l, high[g]))
            x[pl.ds(pl.multiple_of(s * MROWS, MROWS), MROWS)] = value * inverse_count

        k_a = s - HOP * depth

        @pl.when((k_a >= 0) & (k_a < n_chunk))
        def _():
            plain, across_copy = to_inner(k_a)

            @pl.when(has_outer)
            def _():
                plain.wait_recv()
                r = pl.ds(pl.multiple_of(k_a * MROWS, MROWS), MROWS)
                x[r] = x[r] + oin[r]

            @pl.when(middle)
            def _():
                across_copy.start()

            @pl.when(jnp.logical_not(middle))
            def _():
                plain.start()

        k_b = s - b_shift

        @pl.when((k_b >= 0) & (k_b < n_chunk))
        def _():
            to_outer(k_b).wait_recv()

            @pl.when(middle)
            def _():
                r = pl.ds(pl.multiple_of(k_b * MROWS, MROWS), MROWS)
                iin[r] = x[r] + iin[r]

            @pl.when(has_outer)
            def _():
                to_outer(k_b).start()

            to_hbm(k_b).start()

        @pl.when(k_b == ready)
        def _():
            @pl.when(pos == 0)
            def _():
                parts = [iin[k * MROWS:(k + 1) * MROWS] for k in (0, *range(per, per + GROUPS - 1))]
                diag[own] = jnp.concatenate([p[:, :gsize] for p in parts] + [p[:, gsize:] for p in parts], 1)

            def diag_slot(k_d, carry):
                ring_step(diag, dsize, dring, k_d - pos, k_d - start_b, heads_d, k_d - pos, k_d - start_b)
                return carry

            lax.fori_loop(0, heads_d + chips - 1, diag_slot, 0)
            for k in range(heads_d):
                sibling_wait(diag, dsize, dring, k, k)
            r = lax.broadcasted_iota(jnp.int32, (wide, wide), 0)
            c = lax.broadcasted_iota(jnp.int32, (wide, wide), 1)
            inverse[...] = diag[...] + jnp.where(r == c, 1.0, 0.0)

        k_c = k_b - ready - 1
        slab = lax.div(k_c, 2)

        @pl.when((k_c >= 0) & (slab < wide // SLAB) & (lax.rem(k_c, 2) == 0))
        def _():
            mine = pl.ds(pl.multiple_of(slab * SLAB, SLAB), SLAB)
            pair = pl.ds(pl.multiple_of(lax.div(slab, 2) * 2 * SLAB, 2 * SLAB), 2 * SLAB)
            block = inverse[mine, pair]
            block = jnp.where(lax.rem(slab, 2) == 0, block[:, :SLAB], block[:, SLAB:])
            r = lax.broadcasted_iota(jnp.int32, (SLAB, SLAB), 0)
            c = lax.broadcasted_iota(jnp.int32, (SLAB, SLAB), 1)
            start = jnp.concatenate([block, jnp.where(r == c, 1.0, 0.0)], 1)
            work[...] = eliminate(start, 0, SLAB // 2)

        @pl.when((k_c >= 0) & (slab < wide // SLAB) & (lax.rem(k_c, 2) == 1))
        def _():
            slab_update(slab, eliminate(work[...], SLAB // 2, SLAB), inverse, upper)

        return carry

    lax.fori_loop(0, n_chunk + HOP * (n_snp - 1) + 1, slot, 0)
    sibling_wait(heads, HALF, ring, 0, PIECES)
    r = lax.broadcasted_iota(jnp.int32, (wide, wide), 0)
    c = lax.broadcasted_iota(jnp.int32, (wide, wide), 1)
    inverse[...] = jnp.where(r >= c, inverse[...], 0.0)
    out_d = pltpu.make_async_copy(inverse, inverse_hbm, head_sem.at[0])
    out_u = pltpu.make_async_copy(upper, upper_hbm, head_sem.at[2])
    out_u.start()
    out_h = pltpu.make_async_copy(heads, heads_hbm, head_sem.at[1])
    out_d.start()
    out_h.start()

    def finish(k, carry):
        to_inner(k)[0].wait_send()

        @pl.when(has_outer)
        def _():
            to_outer(k).wait_send()

        to_hbm(k).wait()
        return carry

    lax.fori_loop(0, n_chunk, finish, 0)

    def drain_ring(k, carry):
        drain(panels, psize, ring, k, k, (pos > 0) | (k >= PIECES - PACE))
        return carry

    lax.fori_loop(0, PIECES, drain_ring, 0)
    drain(heads, HALF, ring, 0, PIECES)
    for k in range(heads_d):
        drain(diag, dsize, dring, k, k)
    for d in range(1, n_tile):
        count_copy(d).wait_send()
    out_d.wait()
    out_u.wait()
    out_h.wait()


def gather_cross(dosages, phenotypes, n_tile, n_snp):
    rows, snps = dosages.shape
    wide = 2 * BLK
    f32 = jnp.float32
    n_chunk = rows // MROWS * GROUPS
    lanes = wide // GROUPS
    dma = pltpu.SemaphoreType.DMA
    return pl.pallas_call(
        functools.partial(kernel, n_tile, n_snp),
        out_shape=(
            jax.ShapeDtypeStruct((rows, wide), f32),
            jax.ShapeDtypeStruct((wide, wide), f32),
            jax.ShapeDtypeStruct((wide, wide), f32),
            jax.ShapeDtypeStruct((wide, phenotypes.shape[1]), f32),
        ),
        in_specs=[pl.BlockSpec(memory_space=pl.ANY)] * 2,
        out_specs=[pl.BlockSpec(memory_space=pl.ANY)] * 4,
        scratch_shapes=[
            pltpu.VMEM((rows, snps), f32),
            pltpu.VMEM((wide, snps), f32),
            pltpu.VMEM((wide, phenotypes.shape[1]), f32),
            pltpu.VMEM((wide, wide), f32),
            pltpu.VMEM((wide, wide), f32),
            pltpu.VMEM((wide, wide), f32),
            pltpu.VMEM((SLAB, 2 * SLAB), f32),
            pltpu.VMEM((wide, snps), jnp.bfloat16),
            pltpu.VMEM((wide, snps), jnp.bfloat16),
            pltpu.VMEM((n_tile, 1, snps), f32),
            pltpu.VMEM((1, snps), f32),
            pltpu.VMEM((1, snps), f32),
            pltpu.VMEM((rows * GROUPS, lanes), f32),
            pltpu.VMEM((rows * GROUPS, lanes), f32),
            pltpu.VMEM((rows * GROUPS, lanes), f32),
            dma((rows // MROWS,)),
            dma((3,)),
            dma((n_chunk,)),
            dma((n_tile,)),
            dma((n_tile,)),
        ]
        + [dma((PIECES + 1,))] * 8
        + [dma((DIAG_PIECES,))] * 8
        + [dma((n_chunk,))] * 4,
        compiler_params=pltpu.CompilerParams(
            collective_id=0, has_side_effects=True, vmem_limit_bytes=58 * 1024 * 1024
        ),
    )(dosages, phenotypes)


def body(dosages, phenotypes):
    n_tile = lax.axis_size("tile")
    n_snp = lax.axis_size("snp")
    tile_index = lax.axis_index("tile")
    cross, inverse, upper, heads = gather_cross(dosages, phenotypes, n_tile, n_snp)
    near = functools.partial(lax.dot_general, precision=lax.Precision.HIGH, preferred_element_type=jnp.float32)
    wide = 2 * BLK
    ordered = inverse.reshape(wide, 2, GROUPS, BLK // GROUPS).transpose(0, 2, 1, 3).reshape(wide, wide)
    factor = near(cross, ordered, NT)
    lower = upper.T
    solved = jnp.dot(inverse, heads, precision=lax.Precision.HIGHEST)
    head_rows = jnp.where(
        tile_index == 0, lower[:BLK], jnp.where(tile_index == 1, lower[BLK:], factor[:BLK])
    )
    factor = factor.at[:BLK].set(head_rows)
    current = phenotypes - jnp.dot(factor, solved, precision=lax.Precision.HIGH)
    head = jnp.where(tile_index == 0, solved[:BLK], jnp.where(tile_index == 1, solved[BLK:], current[:BLK]))
    return (factor, current.at[:BLK].set(head))


def solution(mesh):
    placed = (P("tile", "snp"), P("tile", "snp"))
    return jax.shard_map(
        body,
        mesh=mesh,
        in_specs=placed,
        out_specs=(P("tile", None), P("tile", "snp")),
        check_vma=False,
    )
```
